128 devices in a mesh: mom: 8 (over y, core), pair: 16 (over x, z).
Axes of the slice: x: 4, y: 4, z: 4, core: 2. Of those that a mesh axis runs over, the one named last changes fastest.
Arguments:
- blocks: bfloat16 [8, 16, 1024, 1024], P('mom', None, 'pair'), may hold values from -1.078125 to 1.078125
- left_ids: int32 [8, 48], P('mom', 'pair'), may hold values from 0 to 15
- right_ids: int32 [8, 48], P('mom', 'pair'), may hold values from 0 to 15
- slice_ids: int32 [8, 48], P('mom', 'pair'), may hold values from 0 to 1
- weight_ids: int32 [8, 48], P('mom', 'pair'), may hold values from 0 to 7
- counts: int32 [8, 16], P('mom', 'pair'), may hold values from 1 to 3, 32 in all within a row
- subduction: float32 [8], replicated, may hold values from -1 to 1
Outputs:
- operator: float32 [8, 1024, 2, 1024], P('mom', 'pair')
The draws below stay inside these ranges and needn't reach their ends.
Inputs may be any that keep to these rules, and one draw needn't show every extreme that they name: Each row of counts sums to exactly 32.
All inputs are finite; a program needn't handle non-finite values. No bound on the sum of `counts` on one device may be relied on, other than what follows from the above.
Results may differ from the reference program's by a relative error of at most 0.0029.
Values may be sent and summed in bfloat16 or wider, within the bound.
A program may use at most 128 MiB of HBM per device.

```python
import math
import jax
import jax.numpy as jnp
import numpy as np
from jax import lax

ORDER = 1024
FAM = 16
PAIR_DEV = 3
SLICES = 2
NW = 8
MOMS = 8
LISTS = 16
PAIRS = 48


def set_ends(values, rng, smallest, high):
    longest = values.shape.index(max(values.shape))
    spots = []
    for shift in (0, 1):
        where = [jax.random.randint(jax.random.fold_in(rng, axis), (), 0, length) for axis, length in enumerate(values.shape)]
        where[longest] = (where[longest] + shift) % values.shape[longest]
        spots.append(tuple(where))
    return values.at[spots[0]].set(smallest).at[spots[1]].set(high)


def block_levels(key, extent, split, least, top_value):
    def one(dim, blocks):
        steps = jax.random.uniform(jax.random.fold_in(jax.random.fold_in(key, 6), dim), (blocks,), jnp.float32, least / len(split), top_value / len(split))
        return jnp.repeat(jnp.exp(steps), extent[dim] // blocks).reshape((-1,) + (1,) * (len(extent) - dim - 1))

    gain = one(*split[0])
    for cut in split[1:]:
        gain = gain * one(*cut)
    return gain


def profile(number_of, total, bound, slope):
    loads = [(1 << 20) // math.isqrt(rank ** slope) + 1 for rank in range(2, number_of + 1)]
    spare, holding = total - bound - (number_of - 1), [1] * (number_of - 1)
    while spare > 0:
        movable = [i for i in range(number_of - 1) if holding[i] < bound]
        whole, left = sum([loads[i] for i in movable]), spare
        for i in movable:
            more = min(bound - holding[i], max(1, left * loads[i] // whole), spare)
            holding[i] = holding[i] + more
            spare = spare - more
    return np.array([bound] + holding)


def uneven(key, amount, total, bound, skew):
    if amount == 2:
        one = jax.random.randint(key, (), max(1, total - bound), min(bound, total - 1) + 1)
        return jnp.stack([one, total - one])
    lengths = jnp.asarray(profile(amount, total, bound, skew), jnp.int32)
    pairs = (amount - 1) // 2
    source_of, sink = lengths[1:1 + 2 * pairs:2], lengths[2:2 + 2 * pairs:2]
    room = jnp.minimum(source_of - 1, bound - sink)
    shifted = jax.random.randint(jax.random.fold_in(key, 1), (pairs,), 0, 1 << 20) % (room + 1)
    lengths = lengths.at[1:1 + 2 * pairs:2].set(source_of - shifted).at[2:2 + 2 * pairs:2].set(sink + shifted)
    return lengths[jax.random.permutation(jax.random.fold_in(key, 2), amount)]


def noise(stream_key, dims, spread, most, cuts=(), held_as=jnp.bfloat16):
    values = jax.random.normal(stream_key, dims, jnp.float32) * spread
    if len(cuts) > 0:
        values = block_levels(stream_key, dims, cuts, -0.22, 0.18) * values
    return jnp.clip(values, min=-most, max=most).astype(held_as)


def setup_inputs(seed: int = 0) -> dict:
    key_of = jax.random.split(jax.random.key(seed), 8)
    blocks = noise(key_of[0], (MOMS, FAM, ORDER, ORDER), 0.18, 1.078125, ((0, 8), (2, 16)))
    left_ids = set_ends(jax.random.randint(key_of[1], (MOMS, PAIRS), 0, FAM), jax.random.fold_in(key_of[1], 1), 0, FAM - 1).astype(jnp.int32)
    right_ids = set_ends(jax.random.randint(key_of[2], (MOMS, PAIRS), 0, FAM), jax.random.fold_in(key_of[2], 1), 0, FAM - 1).astype(jnp.int32)
    slice_ids = set_ends(jax.random.randint(key_of[3], (MOMS, PAIRS), 0, SLICES), jax.random.fold_in(key_of[3], 1), 0, SLICES - 1).astype(jnp.int32)
    weight_ids = set_ends(jax.random.randint(key_of[4], (MOMS, PAIRS), 0, NW), jax.random.fold_in(key_of[4], 1), 0, NW - 1).astype(jnp.int32)
    counts = jax.vmap(lambda own: uneven(own, LISTS, LISTS * (PAIR_DEV - 1), PAIR_DEV, 2))(jax.random.split(key_of[5], MOMS)).reshape((MOMS, LISTS)).astype(jnp.int32)
    subduction = jnp.clip(jax.random.uniform(key_of[6], (NW,), jnp.float32, -1.0, 1.0), -1.0, 1.0)
    return {"blocks": blocks, "left_ids": left_ids, "right_ids": right_ids, "slice_ids": slice_ids, "weight_ids": weight_ids, "counts": counts, "subduction": subduction}


def reference(blocks, left_ids, right_ids, slice_ids, weight_ids, counts, subduction):
    slot = jnp.arange(PAIRS, dtype=jnp.int32)
    fam_ids = jnp.arange(FAM, dtype=jnp.int32)
    outputs = []
    for family in range(MOMS):
        partner = family ^ 1
        limit = counts[family][slot // PAIR_DEV]
        live = (slot % PAIR_DEV) < limit
        weight = subduction[weight_ids[family]]
        select = (slice_ids[family][:, None] == jnp.arange(SLICES, dtype=jnp.int32)[None, :]).astype(jnp.float32)
        coef = jnp.where(live, weight, jnp.zeros_like(weight))[:, None] * select
        right_hot = (right_ids[family][:, None] == fam_ids[None, :]).astype(jnp.float32)
        left_hot = (left_ids[family][:, None] == fam_ids[None, :]).astype(jnp.float32)
        mixing = jnp.einsum("kt,kb,ka->tba", coef, right_hot, left_hot, precision=lax.Precision.HIGHEST)
        own = blocks[family].astype(jnp.float32).reshape(FAM, ORDER * ORDER)
        combined = jnp.dot(mixing.reshape(SLICES * FAM, FAM), own, precision=lax.Precision.HIGHEST)
        combined = combined.astype(jnp.bfloat16).reshape(SLICES, FAM, ORDER, ORDER)
        lefted = jnp.transpose(combined, (2, 0, 1, 3)).reshape(ORDER * SLICES, FAM * ORDER)
        total = jnp.dot(lefted, blocks[partner].reshape(FAM * ORDER, ORDER), preferred_element_type=jnp.float32)
        outputs.append(total.reshape(ORDER, SLICES, ORDER))
    return jnp.stack(outputs)
```

```python
import functools

import jax
import jax.numpy as jnp
from jax import lax
from jax.experimental import pallas as pl
from jax.experimental.pallas import tpu as pltpu
from jax.sharding import PartitionSpec as P

MESH = pl.DeviceIdType.MESH
PAIR_DEV = 3
SLICES = 2
FAM = 16
ROWS = 64
LANES = 128
ORDER = 1024
DEVS = 16
OUT_ROWS = SLICES * ROWS
MIX = SLICES * FAM
SUB = 16
CHUNK = 256
NCHUNK = ORDER // CHUNK

PEERS = ((0, 0), (0, 1), (1, 0), (3, 0), (1, 1), (3, 1), (2, 0), (2, 1))


def kernel(
    left, right, slices, weights, counts, subduction, blocks, out,
    rows_b, parts_a, combined, partial, landed, table, tile, tiles, spread,
    own_sem, tile_send, tile_recv, a_send, a_recv, b_send, b_recv, c_send, c_recv,
):
    mom, pair = lax.axis_index("mom"), lax.axis_index("pair")
    other = mom + 1 - 2 * lax.rem(mom, 2)
    x, z = lax.div(pair, 4), lax.rem(pair, 4)
    odd = lax.rem(z, 2)
    across = pair + 1 - 2 * odd

    def peer(k, sign):
        dx, dz = PEERS[k]
        to_x = lax.rem(x + sign * dx + 4, 4)
        return to_x * 4 + (3 - z if dz else z)

    barrier = pltpu.get_barrier_semaphore()
    for p in range(DEVS):
        pl.semaphore_signal(barrier, 1, device_id=(other, p), device_id_type=MESH)
    pl.semaphore_signal(barrier, 1, device_id=(mom, across), device_id_type=MESH)

    mine = pl.ds(pl.multiple_of(odd * ROWS, ROWS), ROWS)
    own = pltpu.make_async_copy(blocks.at[0], rows_b.at[:, mine, :], own_sem)
    own.start()

    row = lax.broadcasted_iota(jnp.int32, (8, LANES), 0)
    keys = jnp.zeros((8, LANES), jnp.int32)
    coefs = jnp.zeros((8, LANES), jnp.float32)
    for s in range(PAIR_DEV):
        key = (slices[0, s] * FAM + right[0, s]) * FAM + left[0, s]
        coef = jnp.where(s < counts[0, 0], subduction[weights[0, s]], 0.0)
        keys = jnp.where(row == s, key, keys)
        coefs = jnp.where(row == 4 + s, coef, coefs)
    tile[...] = jnp.where(row < 4, keys.astype(jnp.float32), coefs)

    pl.semaphore_wait(barrier, DEVS + 1)
    sends = []
    for p in range(DEVS):
        copy = pltpu.make_async_remote_copy(
            tile, tiles.at[pair], tile_send.at[p], tile_recv.at[pair],
            device_id=(other, p), device_id_type=MESH,
        )
        copy.start()
        sends.append(copy)

    own.wait()
    gets_a = []
    for k in range(len(PEERS)):
        to = peer(k, 1)
        columns = pl.ds(pl.multiple_of(lax.div(to, 2) * LANES, LANES), LANES)
        copy = pltpu.make_async_remote_copy(
            rows_b.at[:, mine, columns], parts_a.at[k], a_send.at[k], a_recv.at[k],
            device_id=(other, to), device_id_type=MESH,
        )
        copy.start()
        sends.append(copy)
        gets_a.append(copy)
    gets_b = []
    for n in range(NCHUNK):
        part = rows_b.at[:, mine, pl.ds(n * CHUNK, CHUNK)]
        copy = pltpu.make_async_remote_copy(
            part, part, b_send.at[n], b_recv.at[n],
            device_id=(mom, across), device_id_type=MESH,
        )
        copy.start()
        sends.append(copy)
        theirs = pl.ds(pl.multiple_of((1 - odd) * ROWS, ROWS), ROWS)
        part = rows_b.at[:, theirs, pl.ds(n * CHUNK, CHUNK)]
        gets_b.append(pltpu.make_async_copy(part, part, b_recv.at[n]))

    place = lax.broadcasted_iota(jnp.int32, (MIX, LANES), 0) * FAM
    place = place + lax.div(lax.broadcasted_iota(jnp.int32, (MIX, LANES), 1), SUB)
    place_lo = place.astype(jnp.float32)
    place_hi = (place + LANES // SUB).astype(jnp.float32)
    lo = jnp.zeros((MIX, LANES), jnp.float32)
    hi = jnp.zeros((MIX, LANES), jnp.float32)
    for p in range(DEVS):
        pltpu.make_async_copy(tile, tiles.at[p], tile_recv.at[p]).wait()
    for p in range(DEVS):
        for s in range(PAIR_DEV):
            key = tiles[p, s : s + 1, :]
            coef = tiles[p, 4 + s : 5 + s, :]
            lo = lo + jnp.where(place_lo == key, coef, 0.0)
            hi = hi + jnp.where(place_hi == key, coef, 0.0)
    rest = jnp.concatenate([lo, hi], axis=1)
    diagonal = lax.broadcasted_iota(jnp.int32, (SUB, FAM * SUB), 0) == lax.rem(
        lax.broadcasted_iota(jnp.int32, (SUB, FAM * SUB), 1), SUB
    )
    for level in range(3):
        part = rest.astype(jnp.bfloat16).astype(jnp.float32)
        rest = rest - part
        spread[level] = part
    for level in range(3):
        for r in range(MIX):
            square = jnp.where(diagonal, spread[level, r : r + 1, :], 0.0)
            table[r * SUB : (r + 1) * SUB, level * FAM * SUB : (level + 1) * FAM * SUB] = (
                square.astype(jnp.bfloat16)
            )

    for k in range(len(PEERS)):
        gets_a[k].wait_recv()

        @pl.loop(0, ROWS // (2 * SUB))
        def _(h):
            base = pl.multiple_of(h * 2 * SUB, 2 * SUB)
            both = parts_a[k, :, pl.ds(base, 2 * SUB), :]
            first = both[:, :SUB, :].reshape(FAM * SUB, LANES)
            second = both[:, SUB:, :].reshape(FAM * SUB, LANES)
            wide = jnp.concatenate([first, second], axis=1)
            mixed = jnp.dot(
                table[...],
                jnp.concatenate([wide, wide, wide], axis=0),
                preferred_element_type=jnp.float32,
            ).astype(jnp.bfloat16)
            for r in range(MIX):
                t, b = divmod(r, FAM)
                for e in range(2):
                    combined[
                        pl.ds(k * OUT_ROWS + t * ROWS + base + e * SUB, SUB),
                        b * LANES : (b + 1) * LANES,
                    ] = mixed[r * SUB : (r + 1) * SUB, e * LANES : (e + 1) * LANES]

    gets_c = {}

    def reduce(n):
        total = jnp.zeros((OUT_ROWS, CHUNK), jnp.float32)
        for k in range(len(PEERS)):
            gets_c[n, k].wait_recv()
            total = total + landed[n, k].astype(jnp.float32)
        out[:, n * CHUNK : (n + 1) * CHUNK] = total

    for n in range(NCHUNK):
        gets_b[n].wait()
        for k in range(len(PEERS)):
            partial[n, k] = jnp.dot(
                combined[k * OUT_ROWS : (k + 1) * OUT_ROWS, :],
                rows_b[:, :, n * CHUNK : (n + 1) * CHUNK].reshape(FAM * LANES, CHUNK),
                preferred_element_type=jnp.float32,
            ).astype(jnp.bfloat16)
            copy = pltpu.make_async_remote_copy(
                partial.at[n, k], landed.at[n, k], c_send.at[n, k], c_recv.at[n, k],
                device_id=(other, peer(k, -1)), device_id_type=MESH,
            )
            copy.start()
            sends.append(copy)
            gets_c[n, k] = copy
        if n > 0:
            reduce(n - 1)
    reduce(NCHUNK - 1)
    for copy in sends:
        copy.wait_send()


def body(blocks, left_ids, right_ids, slice_ids, weight_ids, counts, subduction):
    bf16, f32 = jnp.bfloat16, jnp.float32
    peers = len(PEERS)
    dma = pltpu.SemaphoreType.DMA
    result = pl.pallas_call(
        kernel,
        out_shape=jax.ShapeDtypeStruct((OUT_ROWS, ORDER), f32),
        in_specs=[pl.BlockSpec(memory_space=pltpu.SMEM)] * 6
        + [pl.BlockSpec(memory_space=pl.ANY)],
        out_specs=pl.BlockSpec(memory_space=pltpu.VMEM),
        scratch_shapes=[
            pltpu.VMEM((FAM, 2 * ROWS, ORDER), bf16),
            pltpu.VMEM((peers, FAM, ROWS, LANES), bf16),
            pltpu.VMEM((peers * OUT_ROWS, FAM * LANES), bf16),
            pltpu.VMEM((NCHUNK, peers, OUT_ROWS, CHUNK), bf16),
            pltpu.VMEM((NCHUNK, peers, OUT_ROWS, CHUNK), bf16),
            pltpu.VMEM((MIX * SUB, 3 * FAM * SUB), bf16),
            pltpu.VMEM((8, LANES), f32),
            pltpu.VMEM((DEVS, 8, LANES), f32),
            pltpu.VMEM((3, MIX, FAM * SUB), f32),
            dma, dma((DEVS,)), dma((DEVS,)), dma((peers,)), dma((peers,)),
            dma((NCHUNK,)), dma((NCHUNK,)), dma((NCHUNK, peers)), dma((NCHUNK, peers)),
        ],
        compiler_params=pltpu.CompilerParams(
            collective_id=0, has_side_effects=True, vmem_limit_bytes=60 << 20
        ),
        cost_estimate=pl.CostEstimate(
            flops=8 << 30, bytes_accessed=4 << 20, transcendentals=0
        ),
    )(left_ids, right_ids, slice_ids, weight_ids, counts, subduction, blocks)
    result = jnp.transpose(result.reshape(SLICES, ROWS, ORDER), (1, 0, 2))
    return result[None]


def solution(mesh):
    return jax.shard_map(
        body,
        mesh=mesh,
        in_specs=(
            P("mom", None, "pair", None),
            P("mom", "pair"),
            P("mom", "pair"),
            P("mom", "pair"),
            P("mom", "pair"),
            P("mom", "pair"),
            P(),
        ),
        out_specs=P("mom", "pair", None, None),
        check_vma=False,
    )
```

```python
import functools

import jax
import jax.numpy as jnp
from jax import lax
from jax.experimental import pallas as pl
from jax.experimental.pallas import tpu as pltpu
from jax.sharding import PartitionSpec as P

MESH = pl.DeviceIdType.MESH
PAIR_DEV = 3
SLICES = 2
FAM = 16
ROWS = 64
LANES = 128
ORDER = 1024
DEVS = 16
OUT_ROWS = SLICES * ROWS
MIX = SLICES * FAM
SUB = 16
DOT_ROWS = 256
CHUNKS = ((0, 256), (256, 256), (512, 256), (768, 128), (896, 128))

PEERS = ((0, 0), (0, 1), (1, 0), (3, 0), (2, 0), (1, 1), (3, 1), (2, 1))
SLOT = {peer: k for k, peer in enumerate(PEERS)}


def kernel(
    left_in, right_in, slices_in, weights_in, counts_in, subduction_in, blocks, out,
    left, right, slices, weights, counts, subduction,
    rows_b, parts_a, relay, combined, partial, landed,
    table, tile, tiles, spread,
    small_sem, own_sem, tile_send, tile_recv, a_send, a_recv, relay_send, relay_recv,
    b_send, b_recv, c_send, c_recv,
):
    mom, pair = lax.axis_index("mom"), lax.axis_index("pair")
    other = mom + 1 - 2 * lax.rem(mom, 2)
    x, z = lax.div(pair, 4), lax.rem(pair, 4)
    odd = lax.rem(z, 2)
    across = pair + 1 - 2 * odd

    def at(dx, dz):
        return lax.rem(x + dx + 4, 4) * 4 + (3 - z if dz else z)

    friends = [(other, p) for p in range(DEVS)]
    friends += [(mom, across), (mom, at(0, 1))]
    barrier = pltpu.get_barrier_semaphore()
    for friend in friends:
        pl.semaphore_signal(barrier, 1, device_id=friend, device_id_type=MESH)

    mine = pl.ds(pl.multiple_of(odd * ROWS, ROWS), ROWS)
    theirs = pl.ds(pl.multiple_of((1 - odd) * ROWS, ROWS), ROWS)
    own = pltpu.make_async_copy(blocks.at[0], rows_b.at[:, mine, :], own_sem)
    own.start()
    smalls = [
        pltpu.make_async_copy(src, dst, small_sem.at[i])
        for i, (src, dst) in enumerate(
            (
                (left_in, left), (right_in, right), (slices_in, slices),
                (weights_in, weights), (counts_in, counts), (subduction_in, subduction),
            )
        )
    ]
    for copy in smalls:
        copy.start()
    for copy in smalls:
        copy.wait()

    row = lax.broadcasted_iota(jnp.int32, (8, LANES), 0)
    keys = jnp.zeros((8, LANES), jnp.int32)
    coefs = jnp.zeros((8, LANES), jnp.float32)
    for s in range(PAIR_DEV):
        key = (slices[0, s] * FAM + right[0, s]) * FAM + left[0, s]
        coef = jnp.where(s < counts[0, 0], subduction[weights[0, s]], 0.0)
        keys = jnp.where(row == s, key, keys)
        coefs = jnp.where(row == 4 + s, coef, coefs)
    tile[...] = jnp.where(row < 4, keys.astype(jnp.float32), coefs)

    pl.semaphore_wait(barrier, len(friends))
    sends = []

    def send(src, dst, send_sem, recv_sem, to):
        copy = pltpu.make_async_remote_copy(
            src, dst, send_sem, recv_sem, device_id=to, device_id_type=MESH
        )
        copy.start()
        sends.append(copy)
        return copy

    for p in range(DEVS):
        send(tile, tiles.at[pair], tile_send.at[p], tile_recv.at[pair], (other, p))

    own.wait()
    gets_a, gets_relay, gets_b, gets_c = {}, {}, {}, {}
    for n, (first, width) in enumerate(CHUNKS):
        part = rows_b.at[:, mine, pl.ds(first, width)]
        send(part, part, b_send.at[n], b_recv.at[n], (mom, across))
        part = rows_b.at[:, theirs, pl.ds(first, width)]
        gets_b[n] = pltpu.make_async_copy(part, part, b_recv.at[n])

    for dx, dz in ((1, 1), (3, 1), (2, 1), (0, 1), (1, 0), (3, 0), (2, 0), (0, 0)):
        k = SLOT[dx, dz]
        columns = lax.div(at(dx, dz), 2) * LANES
        src = rows_b.at[:, mine, pl.ds(pl.multiple_of(columns, LANES), LANES)]
        if dx and dz:
            gets_relay[dx] = send(
                src, relay.at[dx - 1], a_send.at[k], relay_recv.at[dx - 1], (other, at(dx, 0))
            )
        else:
            gets_a[k] = send(
                src, parts_a.at[k], a_send.at[k], a_recv.at[k], (other, at(dx, dz))
            )
    place = lax.broadcasted_iota(jnp.int32, (MIX, LANES), 0) * FAM
    place = place + lax.div(lax.broadcasted_iota(jnp.int32, (MIX, LANES), 1), SUB)
    place_lo = place.astype(jnp.float32)
    place_hi = (place + LANES // SUB).astype(jnp.float32)
    lo = jnp.zeros((MIX, LANES), jnp.float32)
    hi = jnp.zeros((MIX, LANES), jnp.float32)
    for p in range(DEVS):
        pltpu.make_async_copy(tile, tiles.at[p], tile_recv.at[p]).wait()
    for p in range(DEVS):
        for s in range(PAIR_DEV):
            key = tiles[p, s : s + 1, :]
            coef = tiles[p, 4 + s : 5 + s, :]
            lo = lo + jnp.where(place_lo == key, coef, 0.0)
            hi = hi + jnp.where(place_hi == key, coef, 0.0)
    rest = jnp.concatenate([lo, hi], axis=1)
    diagonal = lax.broadcasted_iota(jnp.int32, (SUB, FAM * SUB), 0) == lax.rem(
        lax.broadcasted_iota(jnp.int32, (SUB, FAM * SUB), 1), SUB
    )
    for level in range(3):
        part = rest.astype(jnp.bfloat16).astype(jnp.float32)
        rest = rest - part
        spread[level] = part
    for level in range(3):
        for r in range(MIX):
            square = jnp.where(diagonal, spread[level, r : r + 1, :], 0.0)
            table[r * SUB : (r + 1) * SUB, level * FAM * SUB : (level + 1) * FAM * SUB] = (
                square.astype(jnp.bfloat16)
            )

    def combine(k):
        gets_a[k].wait_recv()

        @pl.loop(0, ROWS // (2 * SUB))
        def _(h):
            base = pl.multiple_of(h * 2 * SUB, 2 * SUB)
            both = parts_a[k, :, pl.ds(base, 2 * SUB), :]
            first = both[:, :SUB, :].reshape(FAM * SUB, LANES)
            second = both[:, SUB:, :].reshape(FAM * SUB, LANES)
            wide = jnp.concatenate([first, second], axis=1)
            mixed = jnp.dot(
                table[...],
                jnp.concatenate([wide, wide, wide], axis=0),
                preferred_element_type=jnp.float32,
            ).astype(jnp.bfloat16)
            for r in range(MIX):
                t, b = divmod(r, FAM)
                for e in range(2):
                    combined[
                        pl.ds(k * OUT_ROWS + t * ROWS + base + e * SUB, SUB),
                        b * LANES : (b + 1) * LANES,
                    ] = mixed[r * SUB : (r + 1) * SUB, e * LANES : (e + 1) * LANES]

    def pass_on(dx):
        k = SLOT[dx, 1]
        gets_relay[dx].wait_recv()
        gets_a[k] = send(
            relay.at[dx - 1], parts_a.at[k], relay_send.at[dx - 1], a_recv.at[k],
            (mom, at(0, 1)),
        )

    def multiply(n, k, count):
        first, width = CHUNKS[n]
        columns = slice(first, first + width)
        lines = slice(k * OUT_ROWS, (k + count) * OUT_ROWS)
        partial[lines, columns] = jnp.dot(
            combined[lines, :],
            rows_b[:, :, columns].reshape(FAM * LANES, width),
            preferred_element_type=jnp.float32,
        ).astype(jnp.bfloat16)
        for i in range(k, k + count):
            dx, dz = PEERS[i]
            gets_c[n, i] = send(
                partial.at[pl.ds(i * OUT_ROWS, OUT_ROWS), pl.ds(first, width)],
                landed.at[i, :, pl.ds(first, width)],
                c_send.at[n, i], c_recv.at[n, i], (other, at(-dx, dz)),
            )

    def finish(n):
        first, width = CHUNKS[n]
        columns = slice(first, first + width)
        total = jnp.zeros((OUT_ROWS, width), jnp.float32)
        for k in range(len(PEERS)):
            gets_c[n, k].wait_recv()
            total = total + landed[k, :, columns].astype(jnp.float32)
        for t in range(SLICES):
            out[:, t, columns] = total[t * ROWS : (t + 1) * ROWS, :]

    combine(SLOT[0, 0])
    pass_on(1)
    pass_on(3)
    combine(SLOT[0, 1])
    pass_on(2)
    gets_b[0].wait()
    multiply(0, 0, 2)
    for k in range(2, len(PEERS), 2):
        combine(k)
        combine(k + 1)
        multiply(0, k, 2)
    for n in range(1, len(CHUNKS)):
        gets_b[n].wait()
        for k in range(0, len(PEERS), DOT_ROWS // OUT_ROWS):
            multiply(n, k, DOT_ROWS // OUT_ROWS)
    for n in range(len(CHUNKS)):
        finish(n)
    for copy in sends:
        copy.wait_send()


def body(blocks, left_ids, right_ids, slice_ids, weight_ids, counts, subduction):
    bf16, f32 = jnp.bfloat16, jnp.float32
    peers, chunks = len(PEERS), len(CHUNKS)
    dma = pltpu.SemaphoreType.DMA
    result = pl.pallas_call(
        kernel,
        out_shape=jax.ShapeDtypeStruct((ROWS, SLICES, ORDER), f32),
        in_specs=[pl.BlockSpec(memory_space=pl.ANY)] * 7,
        out_specs=pl.BlockSpec(memory_space=pltpu.VMEM),
        scratch_shapes=[pltpu.SMEM((1, PAIR_DEV), jnp.int32)] * 4
        + [
            pltpu.SMEM((1, 1), jnp.int32),
            pltpu.SMEM(subduction.shape, f32),
            pltpu.VMEM((FAM, 2 * ROWS, ORDER), bf16),
            pltpu.VMEM((peers, FAM, ROWS, LANES), bf16),
            pltpu.VMEM((3, FAM, ROWS, LANES), bf16),
            pltpu.VMEM((peers * OUT_ROWS, FAM * LANES), bf16),
            pltpu.VMEM((peers * OUT_ROWS, ORDER), bf16),
            pltpu.VMEM((peers, OUT_ROWS, ORDER), bf16),
            pltpu.VMEM((MIX * SUB, 3 * FAM * SUB), bf16),
            pltpu.VMEM((8, LANES), f32),
            pltpu.VMEM((DEVS, 8, LANES), f32),
            pltpu.VMEM((3, MIX, FAM * SUB), f32),
            dma((6,)), dma, dma((DEVS,)), dma((DEVS,)), dma((peers,)), dma((peers,)),
            dma((3,)), dma((3,)), dma((chunks,)), dma((chunks,)),
            dma((chunks, peers)), dma((chunks, peers)),
        ],
        compiler_params=pltpu.CompilerParams(
            collective_id=0, has_side_effects=True, vmem_limit_bytes=60 << 20
        ),
        cost_estimate=pl.CostEstimate(
            flops=8 << 30, bytes_accessed=4 << 20, transcendentals=0
        ),
    )(left_ids, right_ids, slice_ids, weight_ids, counts, subduction, blocks)
    return result[None]


def solution(mesh):
    return jax.shard_map(
        body,
        mesh=mesh,
        in_specs=(
            P("mom", None, "pair", None),
            P("mom", "pair"),
            P("mom", "pair"),
            P("mom", "pair"),
            P("mom", "pair"),
            P("mom", "pair"),
            P(),
        ),
        out_specs=P("mom", "pair", None, None),
        check_vma=False,
    )
```

```python
import functools

import jax
import jax.numpy as jnp
from jax import lax
from jax.experimental import pallas as pl
from jax.experimental.pallas import tpu as pltpu
from jax.sharding import PartitionSpec as P

MESH = pl.DeviceIdType.MESH
PAIR_DEV = 3
SLICES = 2
FAM = 16
ROWS = 64
LANES = 128
ORDER = 1024
DEVS = 16
OUT_ROWS = SLICES * ROWS
MIX = SLICES * FAM
SUB = 16
DOT_ROWS = 256
CHUNKS = ((0, 256), (256, 256), (512, 256), (768, 128), (896, 128))

PEERS = ((0, 0), (0, 1), (1, 0), (3, 0), (2, 0), (1, 1), (3, 1), (2, 1))
SLOT = {peer: k for k, peer in enumerate(PEERS)}


def kernel(
    left_in, right_in, slices_in, weights_in, counts_in, subduction_in, blocks, out,
    left, right, slices, weights, counts, subduction,
    rows_b, parts_a, relay, combined, partial, landed,
    table, tile, tiles, spread,
    small_sem, own_sem, tile_send, tile_recv, a_send, a_recv, relay_send, relay_recv,
    b_send, b_recv, c_send, c_recv,
):
    mom, pair = lax.axis_index("mom"), lax.axis_index("pair")
    other = mom + 1 - 2 * lax.rem(mom, 2)
    x, z = lax.div(pair, 4), lax.rem(pair, 4)
    odd = lax.rem(z, 2)
    across = pair + 1 - 2 * odd

    def at(dx, dz):
        return lax.rem(x + dx + 4, 4) * 4 + (3 - z if dz else z)

    friends = [(other, p) for p in range(DEVS)]
    friends += [(mom, across), (mom, at(0, 1))]
    barrier = pltpu.get_barrier_semaphore()
    for friend in friends:
        pl.semaphore_signal(barrier, 1, device_id=friend, device_id_type=MESH)

    mine = pl.ds(pl.multiple_of(odd * ROWS, ROWS), ROWS)
    theirs = pl.ds(pl.multiple_of((1 - odd) * ROWS, ROWS), ROWS)
    own = pltpu.make_async_copy(blocks.at[0], rows_b.at[:, mine, :], own_sem)
    own.start()
    smalls = [
        pltpu.make_async_copy(src, dst, small_sem.at[i])
        for i, (src, dst) in enumerate(
            (
                (left_in, left), (right_in, right), (slices_in, slices),
                (weights_in, weights), (counts_in, counts), (subduction_in, subduction),
            )
        )
    ]
    for copy in smalls:
        copy.start()
    for copy in smalls:
        copy.wait()

    row = lax.broadcasted_iota(jnp.int32, (8, LANES), 0)
    keys = jnp.zeros((8, LANES), jnp.int32)
    coefs = jnp.zeros((8, LANES), jnp.float32)
    for s in range(PAIR_DEV):
        key = (slices[0, s] * FAM + right[0, s]) * FAM + left[0, s]
        coef = jnp.where(s < counts[0, 0], subduction[weights[0, s]], 0.0)
        keys = jnp.where(row == s, key, keys)
        coefs = jnp.where(row == 4 + s, coef, coefs)
    tile[...] = jnp.where(row < 4, keys.astype(jnp.float32), coefs)

    pl.semaphore_wait(barrier, len(friends))
    sends = []

    def send(src, dst, send_sem, recv_sem, to):
        copy = pltpu.make_async_remote_copy(
            src, dst, send_sem, recv_sem, device_id=to, device_id_type=MESH
        )
        copy.start()
        sends.append(copy)
        return copy

    for p in range(DEVS):
        send(tile, tiles.at[pair], tile_send.at[p], tile_recv.at[pair], (other, p))

    own.wait()
    gets_a, gets_relay, gets_b, gets_c = {}, {}, {}, {}
    for n, (first, width) in enumerate(CHUNKS):
        part = rows_b.at[:, mine, pl.ds(first, width)]
        send(part, part, b_send.at[n], b_recv.at[n], (mom, across))
        part = rows_b.at[:, theirs, pl.ds(first, width)]
        gets_b[n] = pltpu.make_async_copy(part, part, b_recv.at[n])

    for dx, dz in ((1, 1), (3, 1), (2, 1), (0, 1), (1, 0), (3, 0), (2, 0), (0, 0)):
        k = SLOT[dx, dz]
        columns = lax.div(at(dx, dz), 2) * LANES
        src = rows_b.at[:, mine, pl.ds(pl.multiple_of(columns, LANES), LANES)]
        if dx and dz:
            gets_relay[dx] = send(
                src, relay.at[dx - 1], a_send.at[k], relay_recv.at[dx - 1], (other, at(dx, 0))
            )
        else:
            gets_a[k] = send(
                src, parts_a.at[k], a_send.at[k], a_recv.at[k], (other, at(dx, dz))
            )
    place = lax.broadcasted_iota(jnp.int32, (MIX, LANES), 0) * FAM
    place = place + lax.div(lax.broadcasted_iota(jnp.int32, (MIX, LANES), 1), SUB)
    place_lo = place.astype(jnp.float32)
    place_hi = (place + LANES // SUB).astype(jnp.float32)
    lo = jnp.zeros((MIX, LANES), jnp.float32)
    hi = jnp.zeros((MIX, LANES), jnp.float32)
    for p in range(DEVS):
        pltpu.make_async_copy(tile, tiles.at[p], tile_recv.at[p]).wait()
    for p in range(DEVS):
        for s in range(PAIR_DEV):
            key = tiles[p, s : s + 1, :]
            coef = tiles[p, 4 + s : 5 + s, :]
            lo = lo + jnp.where(place_lo == key, coef, 0.0)
            hi = hi + jnp.where(place_hi == key, coef, 0.0)
    rest = jnp.concatenate([lo, hi], axis=1)
    diagonal = lax.broadcasted_iota(jnp.int32, (SUB, FAM * SUB), 0) == lax.rem(
        lax.broadcasted_iota(jnp.int32, (SUB, FAM * SUB), 1), SUB
    )
    for level in range(3):
        part = rest.astype(jnp.bfloat16).astype(jnp.float32)
        rest = rest - part
        spread[level] = part
    for level in range(3):
        for r in range(MIX):
            square = jnp.where(diagonal, spread[level, r : r + 1, :], 0.0)
            table[r * SUB : (r + 1) * SUB, level * FAM * SUB : (level + 1) * FAM * SUB] = (
                square.astype(jnp.bfloat16)
            )

    def combine(k):
        gets_a[k].wait_recv()

        @pl.loop(0, ROWS // (2 * SUB))
        def _(h):
            base = pl.multiple_of(h * 2 * SUB, 2 * SUB)
            both = parts_a[k, :, pl.ds(base, 2 * SUB), :]
            first = both[:, :SUB, :].reshape(FAM * SUB, LANES)
            second = both[:, SUB:, :].reshape(FAM * SUB, LANES)
            wide = jnp.concatenate([first, second], axis=1)
            mixed = jnp.dot(
                table[...],
                jnp.concatenate([wide, wide, wide], axis=0),
                preferred_element_type=jnp.float32,
            ).astype(jnp.bfloat16)
            for r in range(MIX):
                t, b = divmod(r, FAM)
                for e in range(2):
                    combined[
                        pl.ds(k * OUT_ROWS + t * ROWS + base + e * SUB, SUB),
                        b * LANES : (b + 1) * LANES,
                    ] = mixed[r * SUB : (r + 1) * SUB, e * LANES : (e + 1) * LANES]

    def pass_on(dx):
        k = SLOT[dx, 1]
        gets_relay[dx].wait_recv()
        gets_a[k] = send(
            relay.at[dx - 1], parts_a.at[k], relay_send.at[dx - 1], a_recv.at[k],
            (mom, at(0, 1)),
        )

    def multiply(n, k, count):
        first, width = CHUNKS[n]
        columns = slice(first, first + width)
        lines = slice(k * OUT_ROWS, (k + count) * OUT_ROWS)
        partial[lines, columns] = jnp.dot(
            combined[lines, :],
            rows_b[:, :, columns].reshape(FAM * LANES, width),
            preferred_element_type=jnp.float32,
        ).astype(jnp.bfloat16)
        for i in range(k, k + count):
            dx, dz = PEERS[i]
            gets_c[n, i] = send(
                partial.at[pl.ds(i * OUT_ROWS, OUT_ROWS), pl.ds(first, width)],
                landed.at[i, :, pl.ds(first, width)],
                c_send.at[n, i], c_recv.at[n, i], (other, at(-dx, dz)),
            )

    def finish(n):
        first, width = CHUNKS[n]
        columns = slice(first, first + width)
        total = jnp.zeros((OUT_ROWS, width), jnp.float32)
        for k in range(len(PEERS)):
            gets_c[n, k].wait_recv()
            total = total + landed[k, :, columns].astype(jnp.float32)
        for t in range(SLICES):
            out[:, t, columns] = total[t * ROWS : (t + 1) * ROWS, :]

    combine(SLOT[0, 0])
    pass_on(1)
    pass_on(3)
    combine(SLOT[0, 1])
    pass_on(2)
    gets_b[0].wait()
    multiply(0, 0, 2)
    for k in range(2, len(PEERS), 2):
        combine(k)
        combine(k + 1)
        multiply(0, k, 2)
    for n in range(1, len(CHUNKS)):
        gets_b[n].wait()
        for k in reversed(range(0, len(PEERS), DOT_ROWS // OUT_ROWS)):
            multiply(n, k, DOT_ROWS // OUT_ROWS)
    for n in range(len(CHUNKS)):
        finish(n)
    for copy in sends:
        copy.wait_send()


def body(blocks, left_ids, right_ids, slice_ids, weight_ids, counts, subduction):
    bf16, f32 = jnp.bfloat16, jnp.float32
    peers, chunks = len(PEERS), len(CHUNKS)
    dma = pltpu.SemaphoreType.DMA
    result = pl.pallas_call(
        kernel,
        out_shape=pltpu.VMEM((ROWS, SLICES, ORDER), f32),
        in_specs=[pl.BlockSpec(memory_space=pl.ANY)] * 7,
        out_specs=pl.BlockSpec(memory_space=pltpu.VMEM),
        scratch_shapes=[pltpu.SMEM((1, PAIR_DEV), jnp.int32)] * 4
        + [
            pltpu.SMEM((1, 1), jnp.int32),
            pltpu.SMEM(subduction.shape, f32),
            pltpu.VMEM((FAM, 2 * ROWS, ORDER), bf16),
            pltpu.VMEM((peers, FAM, ROWS, LANES), bf16),
            pltpu.VMEM((3, FAM, ROWS, LANES), bf16),
            pltpu.VMEM((peers * OUT_ROWS, FAM * LANES), bf16),
            pltpu.VMEM((peers * OUT_ROWS, ORDER), bf16),
            pltpu.VMEM((peers, OUT_ROWS, ORDER), bf16),
            pltpu.VMEM((MIX * SUB, 3 * FAM * SUB), bf16),
            pltpu.VMEM((8, LANES), f32),
            pltpu.VMEM((DEVS, 8, LANES), f32),
            pltpu.VMEM((3, MIX, FAM * SUB), f32),
            dma((6,)), dma, dma((DEVS,)), dma((DEVS,)), dma((peers,)), dma((peers,)),
            dma((3,)), dma((3,)), dma((chunks,)), dma((chunks,)),
            dma((chunks, peers)), dma((chunks, peers)),
        ],
        compiler_params=pltpu.CompilerParams(
            collective_id=0, has_side_effects=True, vmem_limit_bytes=56 << 20
        ),
        cost_estimate=pl.CostEstimate(
            flops=8 << 30, bytes_accessed=4 << 20, transcendentals=0
        ),
    )(left_ids, right_ids, slice_ids, weight_ids, counts, subduction, blocks)
    return result[None]


def solution(mesh):
    return jax.shard_map(
        body,
        mesh=mesh,
        in_specs=(
            P("mom", None, "pair", None),
            P("mom", "pair"),
            P("mom", "pair"),
            P("mom", "pair"),
            P("mom", "pair"),
            P("mom", "pair"),
            P(),
        ),
        out_specs=P("mom", "pair", None, None),
        check_vma=False,
    )
```

```python
import functools

import jax
import jax.numpy as jnp
from jax import lax
from jax.experimental import pallas as pl
from jax.experimental.pallas import tpu as pltpu
from jax.sharding import PartitionSpec as P

MESH = pl.DeviceIdType.MESH
PAIR_DEV = 3
SLICES = 2
FAM = 16
ROWS = 64
LANES = 128
ORDER = 1024
DEVS = 16
OUT_ROWS = SLICES * ROWS
MIX = SLICES * FAM
SUB = 16
DOT_ROWS = 256
CHUNKS = ((0, 256), (256, 256), (512, 256), (768, 128), (896, 128))

PEERS = ((0, 0), (0, 1), (1, 0), (3, 0), (2, 0), (1, 1), (3, 1), (2, 1))
SLOT = {peer: k for k, peer in enumerate(PEERS)}


def kernel(
    left_in, right_in, slices_in, weights_in, counts_in, subduction_in, blocks, out,
    left, right, slices, weights, counts, subduction,
    rows_own, rows_b, parts_a, relay, combined, partial, landed,
    table, tile, tiles, spread,
    small_sem, own_sem, near_send, near_recv, tile_send, tile_recv, a_send, a_recv, relay_send, relay_recv,
    b_send, b_recv, c_send, c_recv,
):
    mom, pair = lax.axis_index("mom"), lax.axis_index("pair")
    other = mom + 1 - 2 * lax.rem(mom, 2)
    x, z = lax.div(pair, 4), lax.rem(pair, 4)
    odd = lax.rem(z, 2)
    across = pair + 1 - 2 * odd

    def at(dx, dz):
        return lax.rem(x + dx + 4, 4) * 4 + (3 - z if dz else z)

    friends = [(mom, lax.rem(pair + step, DEVS)) for step in range(1, DEVS)]
    friends += [(other, pair), (other, across)]
    barrier = pltpu.get_barrier_semaphore()
    for friend in friends:
        pl.semaphore_signal(barrier, 1, device_id=friend, device_id_type=MESH)

    mine = pl.ds(pl.multiple_of(odd * ROWS, ROWS), ROWS)
    theirs = pl.ds(pl.multiple_of((1 - odd) * ROWS, ROWS), ROWS)
    own = pltpu.make_async_copy(blocks.at[0], rows_own, own_sem)
    own.start()
    smalls = [
        pltpu.make_async_copy(src, dst, small_sem.at[i])
        for i, (src, dst) in enumerate(
            (
                (left_in, left), (right_in, right), (slices_in, slices),
                (weights_in, weights), (counts_in, counts), (subduction_in, subduction),
            )
        )
    ]
    for copy in smalls:
        copy.start()
    for copy in smalls:
        copy.wait()

    row = lax.broadcasted_iota(jnp.int32, (8, LANES), 0)
    keys = jnp.zeros((8, LANES), jnp.int32)
    coefs = jnp.zeros((8, LANES), jnp.float32)
    for s in range(PAIR_DEV):
        key = (slices[0, s] * FAM + right[0, s]) * FAM + left[0, s]
        coef = jnp.where(s < counts[0, 0], subduction[weights[0, s]], 0.0)
        keys = jnp.where(row == s, key, keys)
        coefs = jnp.where(row == 4 + s, coef, coefs)
    tile[...] = jnp.where(row < 4, keys.astype(jnp.float32), coefs)

    pl.semaphore_wait(barrier, len(friends))
    sends = []

    def send(src, dst, send_sem, recv_sem, to):
        copy = pltpu.make_async_remote_copy(
            src, dst, send_sem, recv_sem, device_id=to, device_id_type=MESH
        )
        copy.start()
        sends.append(copy)
        return copy

    def keep(src, dst, sem):
        copy = pltpu.make_async_copy(src, dst, sem)
        copy.start()
        return copy

    for step in range(1, DEVS):
        send(
            tile, tiles.at[pair], tile_send.at[step], tile_recv.at[pair],
            (mom, lax.rem(pair + step, DEVS)),
        )
    keep(tile, tiles.at[pair], tile_recv.at[pair])

    own.wait()
    gets_a, gets_relay, gets_b, gets_c = {}, {}, {}, {}
    for n, (first, width) in enumerate(CHUNKS):
        columns = pl.ds(first, width)
        send(
            rows_own.at[:, :, columns], rows_b.at[:, mine, columns], b_send.at[n],
            b_recv.at[n], (other, across),
        )
        part = rows_b.at[:, theirs, columns]
        gets_b[n] = pltpu.make_async_copy(part, part, b_recv.at[n])
    for dx, dz in ((1, 1), (3, 1), (2, 1), (0, 1), (1, 0), (3, 0), (2, 0), (0, 0)):
        k = SLOT[dx, dz]
        columns = lax.div(at(dx, dz), 2) * LANES
        src = rows_own.at[:, :, pl.ds(pl.multiple_of(columns, LANES), LANES)]
        if dx and dz:
            gets_relay[dx] = send(
                src, relay.at[dx - 1], a_send.at[k], relay_recv.at[dx - 1], (mom, at(dx, 0))
            )
        elif dx or dz:
            gets_a[k] = send(
                src, parts_a.at[k], a_send.at[k], a_recv.at[k], (mom, at(dx, dz))
            ).wait_recv
        else:
            gets_a[k] = keep(src, parts_a.at[k], a_recv.at[k]).wait
    near = send(rows_own, rows_b.at[:, mine, :], near_send, near_recv, (other, pair))
    place = lax.broadcasted_iota(jnp.int32, (MIX, LANES), 0) * FAM
    place = place + lax.div(lax.broadcasted_iota(jnp.int32, (MIX, LANES), 1), SUB)
    place_lo = place.astype(jnp.float32)
    place_hi = (place + LANES // SUB).astype(jnp.float32)
    lo = jnp.zeros((MIX, LANES), jnp.float32)
    hi = jnp.zeros((MIX, LANES), jnp.float32)
    for p in range(DEVS):
        pltpu.make_async_copy(tile, tiles.at[p], tile_recv.at[p]).wait()
    for p in range(DEVS):
        for s in range(PAIR_DEV):
            key = tiles[p, s : s + 1, :]
            coef = tiles[p, 4 + s : 5 + s, :]
            lo = lo + jnp.where(place_lo == key, coef, 0.0)
            hi = hi + jnp.where(place_hi == key, coef, 0.0)
    rest = jnp.concatenate([lo, hi], axis=1)
    diagonal = lax.broadcasted_iota(jnp.int32, (SUB, FAM * SUB), 0) == lax.rem(
        lax.broadcasted_iota(jnp.int32, (SUB, FAM * SUB), 1), SUB
    )
    for level in range(3):
        part = rest.astype(jnp.bfloat16).astype(jnp.float32)
        rest = rest - part
        spread[level] = part
    for level in range(3):
        for r in range(MIX):
            square = jnp.where(diagonal, spread[level, r : r + 1, :], 0.0)
            table[r * SUB : (r + 1) * SUB, level * FAM * SUB : (level + 1) * FAM * SUB] = (
                square.astype(jnp.bfloat16)
            )

    def combine(k):
        gets_a[k]()

        @pl.loop(0, ROWS // (2 * SUB))
        def _(h):
            base = pl.multiple_of(h * 2 * SUB, 2 * SUB)
            both = parts_a[k, :, pl.ds(base, 2 * SUB), :]
            first = both[:, :SUB, :].reshape(FAM * SUB, LANES)
            second = both[:, SUB:, :].reshape(FAM * SUB, LANES)
            wide = jnp.concatenate([first, second], axis=1)
            mixed = jnp.dot(
                table[...],
                jnp.concatenate([wide, wide, wide], axis=0),
                preferred_element_type=jnp.float32,
            ).astype(jnp.bfloat16)
            for r in range(MIX):
                t, b = divmod(r, FAM)
                for e in range(2):
                    combined[
                        pl.ds(k * OUT_ROWS + t * ROWS + base + e * SUB, SUB),
                        b * LANES : (b + 1) * LANES,
                    ] = mixed[r * SUB : (r + 1) * SUB, e * LANES : (e + 1) * LANES]

    def pass_on(dx):
        k = SLOT[dx, 1]
        gets_relay[dx].wait_recv()
        gets_a[k] = send(
            relay.at[dx - 1], parts_a.at[k], relay_send.at[dx - 1], a_recv.at[k],
            (mom, at(0, 1)),
        ).wait_recv

    def multiply(n, k, count):
        first, width = CHUNKS[n]
        columns = slice(first, first + width)
        lines = slice(k * OUT_ROWS, (k + count) * OUT_ROWS)
        partial[lines, columns] = jnp.dot(
            combined[lines, :],
            rows_b[:, :, columns].reshape(FAM * LANES, width),
            preferred_element_type=jnp.float32,
        ).astype(jnp.bfloat16)
        for i in range(k, k + count):
            dx, dz = PEERS[i]
            src = partial.at[pl.ds(i * OUT_ROWS, OUT_ROWS), pl.ds(first, width)]
            dst = landed.at[i, :, pl.ds(first, width)]
            if dx or dz:
                gets_c[n, i] = send(
                    src, dst, c_send.at[n, i], c_recv.at[n, i], (mom, at(-dx, dz))
                ).wait_recv
            else:
                gets_c[n, i] = keep(src, dst, c_recv.at[n, i]).wait

    def finish(n):
        first, width = CHUNKS[n]
        columns = slice(first, first + width)
        total = jnp.zeros((OUT_ROWS, width), jnp.float32)
        for k in range(len(PEERS)):
            gets_c[n, k]()
            total = total + landed[k, :, columns].astype(jnp.float32)
        for t in range(SLICES):
            out[:, t, columns] = total[t * ROWS : (t + 1) * ROWS, :]

    combine(SLOT[0, 0])
    pass_on(1)
    pass_on(3)
    combine(SLOT[0, 1])
    pass_on(2)
    near.wait_recv()
    gets_b[0].wait()
    multiply(0, 0, 2)
    for k in range(2, len(PEERS), 2):
        combine(k)
        combine(k + 1)
        multiply(0, k, 2)
    for n in range(1, len(CHUNKS)):
        gets_b[n].wait()
        for k in reversed(range(0, len(PEERS), DOT_ROWS // OUT_ROWS)):
            multiply(n, k, DOT_ROWS // OUT_ROWS)
    for n in range(len(CHUNKS)):
        finish(n)
    for copy in sends:
        copy.wait_send()


def body(blocks, left_ids, right_ids, slice_ids, weight_ids, counts, subduction):
    bf16, f32 = jnp.bfloat16, jnp.float32
    peers, chunks = len(PEERS), len(CHUNKS)
    dma = pltpu.SemaphoreType.DMA
    result = pl.pallas_call(
        kernel,
        out_shape=pltpu.VMEM((ROWS, SLICES, ORDER), f32),
        in_specs=[pl.BlockSpec(memory_space=pl.ANY)] * 7,
        out_specs=pl.BlockSpec(memory_space=pltpu.VMEM),
        scratch_shapes=[pltpu.SMEM((1, PAIR_DEV), jnp.int32)] * 4
        + [
            pltpu.SMEM((1, 1), jnp.int32),
            pltpu.SMEM(subduction.shape, f32),
            pltpu.VMEM((FAM, ROWS, ORDER), bf16),
            pltpu.VMEM((FAM, 2 * ROWS, ORDER), bf16),
            pltpu.VMEM((peers, FAM, ROWS, LANES), bf16),
            pltpu.VMEM((3, FAM, ROWS, LANES), bf16),
            pltpu.VMEM((peers * OUT_ROWS, FAM * LANES), bf16),
            pltpu.VMEM((peers * OUT_ROWS, ORDER), bf16),
            pltpu.VMEM((peers, OUT_ROWS, ORDER), bf16),
            pltpu.VMEM((MIX * SUB, 3 * FAM * SUB), bf16),
            pltpu.VMEM((8, LANES), f32),
            pltpu.VMEM((DEVS, 8, LANES), f32),
            pltpu.VMEM((3, MIX, FAM * SUB), f32),
            dma((6,)), dma, dma, dma, dma((DEVS,)), dma((DEVS,)), dma((peers,)), dma((peers,)),
            dma((3,)), dma((3,)), dma((chunks,)), dma((chunks,)),
            dma((chunks, peers)), dma((chunks, peers)),
        ],
        compiler_params=pltpu.CompilerParams(
            collective_id=0, has_side_effects=True, vmem_limit_bytes=56 << 20
        ),
        cost_estimate=pl.CostEstimate(
            flops=8 << 30, bytes_accessed=4 << 20, transcendentals=0
        ),
    )(left_ids, right_ids, slice_ids, weight_ids, counts, subduction, blocks)
    return result[None]


def solution(mesh):
    return jax.shard_map(
        body,
        mesh=mesh,
        in_specs=(
            P("mom", None, "pair", None),
            P("mom", "pair"),
            P("mom", "pair"),
            P("mom", "pair"),
            P("mom", "pair"),
            P("mom", "pair"),
            P(),
        ),
        out_specs=P("mom", "pair", None, None),
        check_vma=False,
    )
```

```python
import functools

import jax
import jax.numpy as jnp
from jax import lax
from jax.experimental import pallas as pl
from jax.experimental.pallas import tpu as pltpu
from jax.sharding import PartitionSpec as P

MESH = pl.DeviceIdType.MESH
PAIR_DEV = 3
SLICES = 2
FAM = 16
ROWS = 64
LANES = 128
ORDER = 1024
DEVS = 16
OUT_ROWS = SLICES * ROWS
MIX = SLICES * FAM
SUB = 16
DOT_ROWS = 256
CHUNKS = ((0, 256), (256, 256), (512, 256), (768, 128), (896, 128))

PEERS = ((0, 0), (0, 1), (1, 0), (3, 0), (2, 0), (1, 1), (3, 1), (2, 1))
SLOT = {peer: k for k, peer in enumerate(PEERS)}


def kernel(
    left_in, right_in, slices_in, weights_in, counts_in, subduction_in, blocks, out,
    left, right, slices, weights, counts, subduction,
    rows_own, rows_b, parts_a, relay, combined, partial, landed,
    table, tile, tiles, spread,
    small_sem, own_sem, near_send, near_recv, tile_send, tile_recv, a_send, a_recv, relay_send, relay_recv,
    b_send, b_recv, c_send, c_recv,
):
    mom, pair = lax.axis_index("mom"), lax.axis_index("pair")
    other = mom + 1 - 2 * lax.rem(mom, 2)
    x, z = lax.div(pair, 4), lax.rem(pair, 4)
    odd = lax.rem(z, 2)
    across = pair + 1 - 2 * odd

    def at(dx, dz):
        return lax.rem(x + dx + 4, 4) * 4 + (3 - z if dz else z)

    friends = [(mom, lax.rem(pair + step, DEVS)) for step in range(1, DEVS)]
    friends += [(other, pair), (other, across)]
    barrier = pltpu.get_barrier_semaphore()
    for friend in friends:
        pl.semaphore_signal(barrier, 1, device_id=friend, device_id_type=MESH)

    mine = pl.ds(pl.multiple_of(odd * ROWS, ROWS), ROWS)
    theirs = pl.ds(pl.multiple_of((1 - odd) * ROWS, ROWS), ROWS)
    own = pltpu.make_async_copy(blocks.at[0], rows_own, own_sem)
    own.start()
    smalls = [
        pltpu.make_async_copy(src, dst, small_sem.at[i])
        for i, (src, dst) in enumerate(
            (
                (left_in, left), (right_in, right), (slices_in, slices),
                (weights_in, weights), (counts_in, counts), (subduction_in, subduction),
            )
        )
    ]
    for copy in smalls:
        copy.start()
    for copy in smalls:
        copy.wait()

    row = lax.broadcasted_iota(jnp.int32, (8, LANES), 0)
    keys = jnp.zeros((8, LANES), jnp.int32)
    coefs = jnp.zeros((8, LANES), jnp.float32)
    for s in range(PAIR_DEV):
        key = (slices[0, s] * FAM + right[0, s]) * FAM + left[0, s]
        coef = jnp.where(s < counts[0, 0], subduction[weights[0, s]], 0.0)
        keys = jnp.where(row == s, key, keys)
        coefs = jnp.where(row == 4 + s, coef, coefs)
    tile[...] = jnp.where(row < 4, keys.astype(jnp.float32), coefs)

    pl.semaphore_wait(barrier, len(friends))
    sends = []

    def send(src, dst, send_sem, recv_sem, to):
        copy = pltpu.make_async_remote_copy(
            src, dst, send_sem, recv_sem, device_id=to, device_id_type=MESH
        )
        copy.start()
        sends.append(copy)
        return copy

    def keep(src, dst, sem):
        copy = pltpu.make_async_copy(src, dst, sem)
        copy.start()
        return copy

    for step in range(1, DEVS):
        send(
            tile, tiles.at[pair], tile_send.at[step], tile_recv.at[pair],
            (mom, lax.rem(pair + step, DEVS)),
        )
    keep(tile, tiles.at[pair], tile_recv.at[pair])

    own.wait()
    gets_a, gets_relay, gets_b, gets_c = {}, {}, {}, {}
    for n, (first, width) in enumerate(CHUNKS):
        columns = pl.ds(first, width)
        send(
            rows_own.at[:, :, columns], rows_b.at[:, mine, columns], b_send.at[n],
            b_recv.at[n], (other, across),
        )
        part = rows_b.at[:, theirs, columns]
        gets_b[n] = pltpu.make_async_copy(part, part, b_recv.at[n])
    for dx, dz in ((1, 1), (3, 1), (2, 1), (0, 1), (1, 0), (3, 0), (2, 0), (0, 0)):
        k = SLOT[dx, dz]
        columns = lax.div(at(dx, dz), 2) * LANES
        src = rows_own.at[:, :, pl.ds(pl.multiple_of(columns, LANES), LANES)]
        if dx and dz:
            gets_relay[dx] = send(
                src, relay.at[dx - 1], a_send.at[k], relay_recv.at[dx - 1], (mom, at(dx, 0))
            )
        elif dx or dz:
            gets_a[k] = send(
                src, parts_a.at[k], a_send.at[k], a_recv.at[k], (mom, at(dx, dz))
            ).wait_recv
        else:
            gets_a[k] = keep(src, parts_a.at[k], a_recv.at[k]).wait
    near = send(rows_own, rows_b.at[:, mine, :], near_send, near_recv, (other, pair))
    place = lax.broadcasted_iota(jnp.int32, (MIX, LANES), 0) * FAM
    place = place + lax.div(lax.broadcasted_iota(jnp.int32, (MIX, LANES), 1), SUB)
    place_lo = place.astype(jnp.float32)
    place_hi = (place + LANES // SUB).astype(jnp.float32)
    lo = jnp.zeros((MIX, LANES), jnp.float32)
    hi = jnp.zeros((MIX, LANES), jnp.float32)
    for p in range(DEVS):
        pltpu.make_async_copy(tile, tiles.at[p], tile_recv.at[p]).wait()
    for p in range(DEVS):
        for s in range(PAIR_DEV):
            key = tiles[p, s : s + 1, :]
            coef = tiles[p, 4 + s : 5 + s, :]
            lo = lo + jnp.where(place_lo == key, coef, 0.0)
            hi = hi + jnp.where(place_hi == key, coef, 0.0)
    rest = jnp.concatenate([lo, hi], axis=1)
    diagonal = lax.broadcasted_iota(jnp.int32, (SUB, FAM * SUB), 0) == lax.rem(
        lax.broadcasted_iota(jnp.int32, (SUB, FAM * SUB), 1), SUB
    )
    for level in range(3):
        part = rest.astype(jnp.bfloat16).astype(jnp.float32)
        rest = rest - part
        spread[level] = part
    for level in range(3):
        for r in range(MIX):
            square = jnp.where(diagonal, spread[level, r : r + 1, :], 0.0)
            table[r * SUB : (r + 1) * SUB, level * FAM * SUB : (level + 1) * FAM * SUB] = (
                square.astype(jnp.bfloat16)
            )

    def combine(k):
        gets_a[k]()

        @pl.loop(0, ROWS // (2 * SUB))
        def _(h):
            base = pl.multiple_of(h * 2 * SUB, 2 * SUB)
            both = parts_a[k, :, pl.ds(base, 2 * SUB), :]
            first = both[:, :SUB, :].reshape(FAM * SUB, LANES)
            second = both[:, SUB:, :].reshape(FAM * SUB, LANES)
            wide = jnp.concatenate([first, second], axis=1)
            mixed = jnp.dot(
                table[...],
                jnp.concatenate([wide, wide, wide], axis=0),
                preferred_element_type=jnp.float32,
            ).astype(jnp.bfloat16)
            for r in range(MIX):
                t, b = divmod(r, FAM)
                for e in range(2):
                    combined[
                        pl.ds(k * OUT_ROWS + t * ROWS + base + e * SUB, SUB),
                        b * LANES : (b + 1) * LANES,
                    ] = mixed[r * SUB : (r + 1) * SUB, e * LANES : (e + 1) * LANES]

    def pass_on(dx):
        k = SLOT[dx, 1]
        gets_relay[dx].wait_recv()
        gets_a[k] = send(
            relay.at[dx - 1], parts_a.at[k], relay_send.at[dx - 1], a_recv.at[k],
            (mom, at(0, 1)),
        ).wait_recv

    def multiply(n, k, count):
        first, width = CHUNKS[n]
        columns = slice(first, first + width)
        lines = slice(k * OUT_ROWS, (k + count) * OUT_ROWS)
        partial[lines, columns] = jnp.dot(
            combined[lines, :],
            rows_b[:, :, columns].reshape(FAM * LANES, width),
            preferred_element_type=jnp.float32,
        ).astype(jnp.bfloat16)
        for i in range(k, k + count):
            dx, dz = PEERS[i]
            src = partial.at[pl.ds(i * OUT_ROWS, OUT_ROWS), pl.ds(first, width)]
            dst = landed.at[i, :, pl.ds(first, width)]
            if dx or dz:
                gets_c[n, i] = send(
                    src, dst, c_send.at[n, i], c_recv.at[n, i], (mom, at(-dx, dz))
                ).wait_recv
            else:
                gets_c[n, i] = keep(src, dst, c_recv.at[n, i]).wait

    def finish(n):
        first, width = CHUNKS[n]
        columns = slice(first, first + width)
        total = jnp.zeros((OUT_ROWS, width), jnp.float32)
        for k in range(len(PEERS)):
            gets_c[n, k]()
            total = total + landed[k, :, columns].astype(jnp.float32)
        for t in range(SLICES):
            out[:, t, columns] = total[t * ROWS : (t + 1) * ROWS, :]

    combine(SLOT[0, 0])
    pass_on(1)
    pass_on(3)
    combine(SLOT[0, 1])
    pass_on(2)
    near.wait_recv()
    gets_b[0].wait()
    multiply(0, 0, 2)
    for k in range(2, len(PEERS), 2):
        combine(k)
        combine(k + 1)
        multiply(0, k, 2)
        if k == 4:
            gets_b[1].wait()
            multiply(1, 0, 2)
            multiply(1, 2, 2)
    for n in range(1, len(CHUNKS)):
        if n > 1:
            gets_b[n].wait()
        for k in reversed(range(0 if n > 1 else 4, len(PEERS), DOT_ROWS // OUT_ROWS)):
            multiply(n, k, DOT_ROWS // OUT_ROWS)
    for n in range(len(CHUNKS)):
        finish(n)
    for copy in sends:
        copy.wait_send()


def body(blocks, left_ids, right_ids, slice_ids, weight_ids, counts, subduction):
    bf16, f32 = jnp.bfloat16, jnp.float32
    peers, chunks = len(PEERS), len(CHUNKS)
    dma = pltpu.SemaphoreType.DMA
    result = pl.pallas_call(
        kernel,
        out_shape=pltpu.VMEM((ROWS, SLICES, ORDER), f32),
        in_specs=[pl.BlockSpec(memory_space=pl.ANY)] * 7,
        out_specs=pl.BlockSpec(memory_space=pltpu.VMEM),
        scratch_shapes=[pltpu.SMEM((1, PAIR_DEV), jnp.int32)] * 4
        + [
            pltpu.SMEM((1, 1), jnp.int32),
            pltpu.SMEM(subduction.shape, f32),
            pltpu.VMEM((FAM, ROWS, ORDER), bf16),
            pltpu.VMEM((FAM, 2 * ROWS, ORDER), bf16),
            pltpu.VMEM((peers, FAM, ROWS, LANES), bf16),
            pltpu.VMEM((3, FAM, ROWS, LANES), bf16),
            pltpu.VMEM((peers * OUT_ROWS, FAM * LANES), bf16),
            pltpu.VMEM((peers * OUT_ROWS, ORDER), bf16),
            pltpu.VMEM((peers, OUT_ROWS, ORDER), bf16),
            pltpu.VMEM((MIX * SUB, 3 * FAM * SUB), bf16),
            pltpu.VMEM((8, LANES), f32),
            pltpu.VMEM((DEVS, 8, LANES), f32),
            pltpu.VMEM((3, MIX, FAM * SUB), f32),
            dma((6,)), dma, dma, dma, dma((DEVS,)), dma((DEVS,)), dma((peers,)), dma((peers,)),
            dma((3,)), dma((3,)), dma((chunks,)), dma((chunks,)),
            dma((chunks, peers)), dma((chunks, peers)),
        ],
        compiler_params=pltpu.CompilerParams(
            collective_id=0, has_side_effects=True, vmem_limit_bytes=56 << 20
        ),
        cost_estimate=pl.CostEstimate(
            flops=8 << 30, bytes_accessed=4 << 20, transcendentals=0
        ),
    )(left_ids, right_ids, slice_ids, weight_ids, counts, subduction, blocks)
    return result[None]


def solution(mesh):
    return jax.shard_map(
        body,
        mesh=mesh,
        in_specs=(
            P("mom", None, "pair", None),
            P("mom", "pair"),
            P("mom", "pair"),
            P("mom", "pair"),
            P("mom", "pair"),
            P("mom", "pair"),
            P(),
        ),
        out_specs=P("mom", "pair", None, None),
        check_vma=False,
    )
```
